32 devices in a mesh: gx: 8 (over z, y), gy: 4 (over x, core).
Axes of the slice: x: 2, y: 2, z: 4, core: 2. Of those that a mesh axis runs over, the one named last changes fastest.
Arguments:
- load_vectors: float32 [8, 4, 8, 8, 192], P('gx', 'gy'), may hold values from -45 to 45
- bond_stiffness: bfloat16 [8, 4, 8, 13, 36864], P('gx', 'gy'), may hold values from 0 to 0.0016937256
- intact_words: int32 [8, 4, 8, 13, 64, 4], P('gx', 'gy'), may hold values from 0 to 65535
- block_cols: int32 [8, 4, 8, 13], P('gx', 'gy'), may hold values from 0 to 89, as said below
- self_stiffness: bfloat16 [8, 4, 8, 36864], P('gx', 'gy'), may hold values from -0.01 to 3.01, as said below
- block_inverse: float32 [8, 4, 8, 36864], P('gx', 'gy'), may hold values from -0.01 to 0.61, as said below
- coarse_basis: float32 [8, 4, 16, 8, 192], P('gx', 'gy'), may hold values from -0.3 to 0.3
- coarse_factor: float32 [512, 512], P(('gx', 'gy')), may hold values from -0.5 to 0.5
Outputs:
- displacement: float32 [8, 4, 8, 8, 192], P('gx', 'gy')
- residual: float32 [8, 4, 8, 8, 192], P('gx', 'gy')
The draws below stay inside these ranges and needn't reach their ends.
Inputs may be any that keep to these rules, and one draw needn't show every extreme that they name: `block_cols`: the 13 codes of a block name different blocks among the 26 around it (never the block itself), each |a - 1|, |c - 1|, |w - 1 - z| at most 1. `self_stiffness`: each block, read as a matrix, is symmetric. `block_inverse`: each block, read as a matrix, is symmetric.
All inputs are finite; a program needn't handle non-finite values.
Results may differ from the reference program's by a relative error of at most 0.0055.
Values may be sent and summed in bfloat16 or wider, within the bound.
A program may use at most 128 MiB of HBM per device.

```python
import math
import jax
import jax.numpy as jnp
from jax import lax

COMP = 3
PB = 64
DOF = 192
WORDS = 4
NS = 13
BZ = 8
NLOAD = 8
CVD = 16
ITERS = 2
NBX = 8
NBY = 4
CV = 512


def draw_load_vectors(key, part):
    shape = (NBX, NBY, BZ, NLOAD, DOF)
    order = jnp.arange(NBX, dtype=jnp.float32)[:, None] * NBY + jnp.arange(NBY, dtype=jnp.float32)[None, :]
    fraction = order / max(NBX * NBY - 1, 1)
    key_one = jax.random.fold_in(key, 0)
    growth = 3.0 ** (0.5 * fraction)
    sample = jnp.clip(jax.random.normal(key_one, shape, jnp.float32), -5.0, 5.0) + 0.6
    return sample * growth[:, :, None, None, None]


def symmetric_blocks(key, spread, lower, upper):
    key_one, key_two = jax.random.split(key)
    shape = (NBX, NBY, BZ, DOF, DOF)
    noise = jax.random.uniform(key_one, shape, jnp.float32, -1.0, 1.0) * (spread / DOF)
    paired = noise + jnp.swapaxes(noise, -1, -2)
    middle = jnp.exp(jax.random.uniform(key_two, (NBX, NBY, BZ, DOF), jnp.float32, math.log(lower), math.log(upper)))
    full = paired + jnp.eye(DOF, dtype=jnp.float32) * middle[..., None, :]
    return full.reshape(NBX, NBY, BZ, DOF * DOF)


def draw_self_stiffness(key, part):
    return symmetric_blocks(jax.random.fold_in(key, 11), 0.3, 1.0, 3.0).astype(jnp.bfloat16)


def draw_block_inverse(key, part):
    return symmetric_blocks(jax.random.fold_in(key, 23), 0.08, 0.2, 0.6)


def draw_block_cols(key, part):
    count = NBX * NBY * BZ
    subkeys = jax.random.split(jax.random.fold_in(key, 37), count)
    orders = jax.vmap(lambda single: jax.random.permutation(single, 26))(subkeys)
    chosen = orders[:, :NS].astype(jnp.int32)
    beside_all = chosen + (chosen >= 13).astype(jnp.int32)
    height = (jnp.arange(count, dtype=jnp.int32) % BZ)[:, None]
    depth_span = BZ + 2
    codes = beside_all // 9 * (3 * depth_span) + beside_all // 3 % 3 * depth_span + height + beside_all % 3
    return codes.reshape(NBX, NBY, BZ, NS).astype(jnp.int32)


def touch_ends(values, key, low, top_value):
    index_at = [jax.random.randint(jax.random.fold_in(key, axis), (), 0, length) for axis, length in enumerate(values.shape)]
    widest = values.shape.index(max(values.shape))
    neighbour = index_at[:widest] + [(index_at[widest] + 1) % values.shape[widest]] + index_at[widest + 1:]
    return values.at[tuple(index_at)].set(low).at[tuple(neighbour)].set(top_value)


def with_spikes(array, stream_key, source, target, parts, factor):
    owner, partner = [(jnp.arange(array.shape[position]) // (array.shape[position] // parts)).reshape([-1 if axis == position else 1 for axis in range(array.ndim)]) for position in (source, target)]
    chosen = jax.random.permutation(stream_key, parts)[partner]
    strong = (owner == chosen) | (owner == (partner + parts // 2) % parts)
    return jnp.where(strong, factor * array, array)


def steps_of(own_key, dims, cuts, least, high):
    loudness = 1.0
    for dim, shards_of in cuts:
        draws = jax.random.uniform(jax.random.fold_in(jax.random.fold_in(own_key, 6), dim), (shards_of,), jnp.float32, least / len(cuts), high / len(cuts))
        loudness = loudness * jnp.repeat(jnp.exp(draws), dims[dim] // shards_of).reshape((-1,) + (1,) * (len(dims) - 1 - dim))
    return loudness


def gaussian(key, extent, width, reach, shards=(), held_as=jnp.bfloat16):
    drawn = width * jax.random.normal(key, extent, jnp.float32)
    if shards:
        drawn = drawn * steps_of(key, extent, shards, -0.22, 0.18)
    return jnp.clip(drawn, -reach, reach).astype(held_as)


def gaussian_with(rng, shape, deviation, reach, cuts, heavy, kind=jnp.bfloat16):
    result = deviation * jax.random.normal(rng, shape, jnp.float32)
    if cuts:
        result = result * steps_of(rng, shape, cuts, -0.22, 0.18)
    return jnp.clip(with_spikes(result, jax.random.fold_in(rng, 3), *heavy), -reach, reach).astype(kind)


def setup_inputs(seed: int = 0) -> dict:
    streams_of = jax.random.split(jax.random.key(seed), 9)
    load_vectors = draw_load_vectors(jax.random.fold_in(streams_of[8], 71), 0)
    bond_stiffness = jnp.clip(0.0016937256 * jax.random.uniform(streams_of[1], (NBX, NBY, BZ, NS, DOF * DOF), jnp.float32) ** steps_of(streams_of[1], (NBX, NBY, BZ, NS, DOF * DOF), ((0, 8), (1, 4)), -0.2, 0.2), 0.0, 0.0016937256).astype(jnp.bfloat16)
    intact_words = touch_ends(jax.random.randint(streams_of[2], (NBX, NBY, BZ, NS, PB, WORDS), 0, 65536), jax.random.fold_in(streams_of[2], 1), 0, 65535).astype(jnp.int32)
    block_cols = draw_block_cols(jax.random.fold_in(streams_of[8], 71), 0)
    self_stiffness = draw_self_stiffness(jax.random.fold_in(streams_of[8], 71), 0)
    block_inverse = draw_block_inverse(jax.random.fold_in(streams_of[8], 71), 0)
    coarse_basis = gaussian(streams_of[6], (NBX, NBY, CVD, BZ, DOF), 0.05, 0.3, ((0, 8), (1, 4)), jnp.float32)
    coarse_factor = gaussian_with(streams_of[7], (CV, CV), CV ** -0.5, 0.5, ((0, 32),), (0, 1, 32, 2.75), jnp.float32)
    return dict(load_vectors=load_vectors, bond_stiffness=bond_stiffness, intact_words=intact_words, block_cols=block_cols, self_stiffness=self_stiffness, block_inverse=block_inverse, coarse_basis=coarse_basis, coarse_factor=coarse_factor)


highest = lax.Precision.HIGHEST


def unpack_bits(packed):
    shifts = jnp.arange(16, dtype=jnp.int32)
    bitset = jnp.right_shift(packed[..., None], shifts) & 1
    return bitset.reshape(packed.shape[:-1] + (packed.shape[-1] * 16,))


def masked_blocks(stiffness, packed):
    intact = unpack_bits(packed).astype(stiffness.dtype)
    leading = stiffness.shape[:-1]
    shaped = stiffness.reshape(leading + (COMP, PB, COMP, PB))
    masked = shaped * intact[..., None, :, None, :]
    return masked.reshape(leading + (DOF, DOF))


def decode_cols(block_cols):
    depth_span = BZ + 2
    return block_cols // (3 * depth_span), (block_cols // depth_span) % 3, block_cols % depth_span


def apply_operator(vector_in, bond_stiffness, intact_words, block_cols, self_stiffness):
    padded = jnp.pad(vector_in, ((1, 1), (1, 1), (1, 1), (0, 0), (0, 0)))
    shift_rows, shift_cols, depth_idx = decode_cols(block_cols)
    across = jnp.arange(NBY, dtype=jnp.int32)[:, None, None]

    def one_row(row_items):
        row_index, stiff_row, packed_row, rows_r, cols_r, depth_r, self_row = row_items
        weights = masked_blocks(stiff_row, packed_row).astype(jnp.float32)
        own_part = vector_in[row_index].astype(jnp.float32)
        ghosts = padded[row_index + rows_r, across + cols_r, depth_r].astype(jnp.float32)
        row_total = jnp.sum(weights, axis=(2, 4))
        column_total = jnp.sum(weights, axis=3)
        forward = row_total[:, :, None, :] * own_part - jnp.einsum('ybsij,ybslj->ybli', weights, ghosts, precision=highest)
        backward = column_total[:, :, :, None, :] * ghosts - jnp.einsum('ybsij,ybli->ybslj', weights, own_part, precision=highest)
        self_matrix = self_row.reshape(NBY, BZ, DOF, DOF).astype(jnp.float32)
        diagonal = jnp.einsum('ybij,yblj->ybli', self_matrix, own_part, precision=highest)
        return forward + diagonal, backward

    rows_out, partial_value = lax.map(one_row, (jnp.arange(NBX, dtype=jnp.int32), bond_stiffness, intact_words, shift_rows, shift_cols, depth_idx, self_stiffness))
    target_rows = jnp.arange(NBX, dtype=jnp.int32)[:, None, None, None] + shift_rows
    target_cols = jnp.arange(NBY, dtype=jnp.int32)[None, :, None, None] + shift_cols
    pooled = jnp.zeros((NBX + 2, NBY + 2, BZ + 2, NLOAD, DOF), jnp.float32)
    pooled = pooled.at[target_rows, target_cols, depth_idx].add(partial_value)
    return rows_out + pooled[1:-1, 1:-1, 1:-1]


def precondition(residual, block_inverse, coarse_basis, coarse_factor):
    inverse = block_inverse.reshape(NBX, NBY, BZ, DOF, DOF)
    own_part = jnp.einsum('xybij,xyblj->xybli', inverse, residual, precision=highest)
    restricted = jnp.einsum('xykbi,xybli->lxyk', coarse_basis, residual, precision=highest).reshape(NLOAD, CV)
    summed = jnp.dot(restricted, coarse_factor, precision=highest)
    spread = jnp.dot(summed, coarse_factor.T, precision=highest).reshape(NLOAD, NBX, NBY, CVD)
    return own_part + jnp.einsum('xykbi,lxyk->xybli', coarse_basis, spread, precision=highest)


def reference(load_vectors, bond_stiffness, intact_words, block_cols, self_stiffness, block_inverse, coarse_basis, coarse_factor):
    solution = jnp.zeros_like(load_vectors)
    residual = load_vectors
    smoothed = precondition(residual, block_inverse, coarse_basis, coarse_factor)
    direction = smoothed
    energy = jnp.sum(residual * smoothed, axis=(0, 1, 2, 4))
    for iteration in range(ITERS):
        rounded = lax.optimization_barrier(direction.astype(jnp.bfloat16))
        operator_out = apply_operator(rounded, bond_stiffness, intact_words, block_cols, self_stiffness)
        step_size = energy / jnp.sum(direction * operator_out, axis=(0, 1, 2, 4))
        step_scale = step_size[None, None, None, :, None]
        solution = solution + step_scale * direction
        residual = residual - step_scale * operator_out
        if iteration + 1 < ITERS:
            smoothed = precondition(residual, block_inverse, coarse_basis, coarse_factor)
            new_energy = jnp.sum(residual * smoothed, axis=(0, 1, 2, 4))
            direction = smoothed + (new_energy / energy)[None, None, None, :, None] * direction
            energy = new_energy
    return solution, residual
```

```python
import functools

import jax
import jax.numpy as jnp
from jax import lax
from jax.experimental import pallas as pl
from jax.experimental.pallas import tpu as pltpu
from jax.sharding import PartitionSpec as P

DOF = 192
HALF = 96
PAIR = 384
NS = 13
BZ = 8
NLOAD = 8
ROWS = BZ * NLOAD
ITERS = 2
SPAN = BZ + 2
GHOSTS = 9 * SPAN
SLOTS = NS + 1
HI = lax.Precision.HIGHEST
F32 = jnp.float32
BF16 = jnp.bfloat16
MESH = pl.DeviceIdType.MESH


def iota(shape, axis):
    return lax.broadcasted_iota(jnp.int32, shape, axis)


def dot(a, b, precision=None):
    return lax.dot_general(
        a, b, (((1,), (0,)), ((), ())), precision=precision, preferred_element_type=F32
    )


def dot_t(a, b, precision=None):
    return lax.dot_general(
        a, b, (((1,), (1,)), ((), ())), precision=precision, preferred_element_type=F32
    )


def prepare_kernel(bond, flags, self_flat, inv_flat, w_out, col_out, row_out, self_out, inv_out, scr):
    step = pl.program_id(0)

    def spread(read):
        @pl.loop(0, 36)
        def _(k8):
            for u in range(8):
                k = k8 * 8 + u
                scr[pl.ds(pl.multiple_of(k * 8, 8), 8), :] = read(pl.ds(pl.multiple_of(k * 128, 128), 128))

    @pl.when(step == 0)
    def _():
        row_out[...] = jnp.zeros_like(row_out)
        spread(lambda lanes: inv_flat[:, lanes])
        for z in range(BZ):
            for t in range(3):
                inv_out[z, :, t * 128 : (t + 1) * 128] = scr[pl.ds(t * 8 + z, HALF, stride=24), :]
        spread(lambda lanes: self_flat[:, lanes].astype(F32))
        for z in range(BZ):
            for t in range(3):
                self_out[z, :, t * 128 : (t + 1) * 128] = scr[
                    pl.ds(t * 8 + z, HALF, stride=24), :
                ].astype(BF16)

    spread(lambda lanes: bond[0, :, lanes].astype(F32))
    lane = iota((16, PAIR), 1)
    column = lane % DOF % 64
    code = (lane // DOF) * 8 + (column // 16) * 2 + (column % 16) // 8
    picker = (code == iota((16, PAIR), 0)).astype(BF16)
    picked = dot(flags[0], picker).astype(jnp.int32)
    lane_bit = jnp.left_shift(1, iota((1, PAIR), 1) % DOF % 8)
    keep = jnp.where((picked & lane_bit) != 0, 1.0, 0.0).astype(F32)
    for z in range(BZ):
        for t in range(3):
            lanes = slice(t * 128, (t + 1) * 128)
            mask = keep[z * 32 : (z + 1) * 32, lanes]
            part = scr[pl.ds(t * 8 + z, HALF, stride=24), :] * jnp.concatenate([mask] * 3, axis=0)
            w_out[z, :, lanes] = part.astype(BF16)
            row_out[z, :, lanes] += part
            col_out[0, z : z + 1, lanes] = jnp.sum(part, axis=0, keepdims=True)


def prepare(bond, flags, self_flat, inv_flat):
    whole = lambda *shape: pl.BlockSpec(shape, lambda s: (0,) * len(shape))
    return pl.pallas_call(
        prepare_kernel,
        grid=(NS,),
        in_specs=[
            pl.BlockSpec((1, BZ, DOF * DOF), lambda s: (s, 0, 0)),
            pl.BlockSpec((1, 256, 16), lambda s: (s, 0, 0)),
            whole(BZ, DOF * DOF),
            whole(BZ, DOF * DOF),
        ],
        out_specs=[
            pl.BlockSpec((BZ, HALF, PAIR), lambda s: (0, 0, s)),
            pl.BlockSpec((1, BZ, PAIR), lambda s: (s, 0, 0)),
            whole(BZ, HALF, PAIR),
            whole(BZ, HALF, PAIR),
            whole(BZ, HALF, PAIR),
        ],
        out_shape=[
            jax.ShapeDtypeStruct((BZ, HALF, NS * PAIR), BF16),
            jax.ShapeDtypeStruct((NS, BZ, PAIR), F32),
            jax.ShapeDtypeStruct((BZ, HALF, PAIR), F32),
            jax.ShapeDtypeStruct((BZ, HALF, PAIR), BF16),
            jax.ShapeDtypeStruct((BZ, HALF, PAIR), F32),
        ],
        scratch_shapes=[pltpu.VMEM((288 * 8, 128), F32)],
        compiler_params=pltpu.CompilerParams(vmem_limit_bytes=40 * 1024 * 1024),
        name="prepare",
    )(bond, flags, self_flat, inv_flat)


def main_kernel(
    nx,
    ny,
    codes,
    pool_at,
    load,
    w_hbm,
    col_in,
    row_in,
    self_in,
    inv_in,
    basis,
    factor,
    disp_out,
    res_out,
    w,
    col,
    row_sum,
    ghost,
    wide,
    lhs,
    terms,
    back_send,
    back_recv,
    sum_y,
    sum_x,
    image,
    even_img,
    odd_img,
    w_sem,
    halo_send_sem,
    halo_recv_sem,
    back_send_sem,
    back_recv_sem,
    y_send_sem,
    y_recv_sem,
    x_send_sem,
    x_recv_sem,
):
    cv = factor.shape[1]
    me_x, me_y = lax.axis_index("gx"), lax.axis_index("gy")

    def neighbour(n):
        x, y = me_x + n // 3 - 1, me_y + n % 3 - 1
        return x, y, (x >= 0) & (x < nx) & (y >= 0) & (y < ny)

    others = [n for n in range(9) if n != 4]
    load_w = pltpu.make_async_copy(w_hbm, w, w_sem)
    load_w.start()
    barrier = pltpu.get_barrier_semaphore()
    for n in others:
        x, y, there = neighbour(n)

        @pl.when(there)
        def _():
            pl.semaphore_signal(barrier, inc=1, device_id=(x, y), device_id_type=MESH)

    for off in range(1, ny):
        pl.semaphore_signal(
            barrier, inc=1, device_id=(me_x, lax.rem(me_y + off, ny)), device_id_type=MESH
        )
    for off in range(1, nx):
        pl.semaphore_signal(
            barrier, inc=1, device_id=(lax.rem(me_x + off, nx), me_y), device_id_type=MESH
        )

    def wait_barrier():
        peers = nx + ny - 2
        for n in others:
            peers = peers + neighbour(n)[2].astype(jnp.int32)
        pl.semaphore_wait(barrier, peers)

    to_even = (iota((DOF, HALF), 0) == 2 * iota((DOF, HALF), 1)).astype(F32)
    to_odd = (iota((DOF, HALF), 0) == 2 * iota((DOF, HALF), 1) + 1).astype(F32)
    from_even = (iota((HALF, DOF), 1) == 2 * iota((HALF, DOF), 0)).astype(F32)
    from_odd = (iota((HALF, DOF), 1) == 2 * iota((HALF, DOF), 0) + 1).astype(F32)
    lane = iota((NLOAD, 128), 1)

    def per_load(product):
        total = jnp.sum(product.reshape(BZ, NLOAD, DOF), axis=0)
        return jnp.sum(total, axis=1, keepdims=True)

    def smooth(field):
        even, odd = dot(field, to_even, HI), dot(field, to_odd, HI)
        out = []
        for z in range(BZ):
            rows = slice(z * NLOAD, (z + 1) * NLOAD)
            both = jnp.concatenate([even[rows], odd[rows]], axis=0)
            product = dot(both, inv_in[z], HI)
            out.append((product[:NLOAD] + pltpu.roll(product[NLOAD:], DOF, 1))[:, :DOF])
        return jnp.concatenate(out, axis=0)

    def restrict(field):
        total = None
        for z in range(BZ):
            part = dot_t(field[z * NLOAD : (z + 1) * NLOAD], basis[z], HI)
            total = part if total is None else total + part
        return dot(total, factor[...], HI)

    def prolong(t):
        spread = dot_t(t, factor[...], HI)
        return jnp.concatenate([dot(spread, basis[z], HI) for z in range(BZ)], axis=0)

    def pack(values):
        out = jnp.zeros((NLOAD, 128), F32)
        for k, value in enumerate(values):
            out = jnp.where(lane == k, value, out)
        return out

    def pick(packed, k):
        return jnp.sum(jnp.where(lane == k, packed, 0.0), axis=1, keepdims=True)

    def all_sum(turn, width):
        for buf, send_sem, recv_sem, me, size, axis in (
            (sum_y, y_send_sem, y_recv_sem, me_y, ny, 1),
            (sum_x, x_send_sem, x_recv_sem, me_x, nx, 0),
        ):
            copies = []
            for off in range(1, size):
                to = lax.rem(me + off, size)
                slot = buf.at[turn, me, :, pl.ds(0, width)]
                copy = pltpu.make_async_remote_copy(
                    src_ref=slot,
                    dst_ref=slot,
                    send_sem=send_sem.at[turn, off - 1],
                    recv_sem=recv_sem.at[turn, off - 1],
                    device_id=(me_x, to) if axis == 1 else (to, me_y),
                    device_id_type=MESH,
                )
                copy.start()
                copies.append(copy)
            for copy in copies:
                copy.wait_recv()
            for copy in copies:
                copy.wait_send()
            total = buf[turn, 0, :, :width]
            for j in range(1, size):
                total = total + buf[turn, j, :, :width]
            if axis == 1:
                sum_x[turn, me_x, :, :width] = total
        return total

    def exchange(turn, src, dst, send_sem, recv_sem):
        def copy_to(n):
            x, y, there = neighbour(n)
            copy = pltpu.make_async_remote_copy(
                src_ref=src(n),
                dst_ref=dst.at[turn, 8 - n],
                send_sem=send_sem.at[turn, n],
                recv_sem=recv_sem.at[turn, 8 - n],
                device_id=(x, y),
                device_id_type=MESH,
            )
            return copy, there

        def start(n):
            copy, there = copy_to(n)
            pl.when(there)(copy.start)

        def finish_recv(n):
            x, y, there = neighbour(n)
            arriving = pltpu.make_async_remote_copy(
                src_ref=src(n),
                dst_ref=dst.at[turn, n],
                send_sem=send_sem.at[turn, n],
                recv_sem=recv_sem.at[turn, n],
                device_id=(x, y),
                device_id_type=MESH,
            )
            pl.when(there)(arriving.wait_recv)

        def finish_send(n):
            copy, there = copy_to(n)
            pl.when(there)(copy.wait_send)

        return start, finish_recv, finish_send

    residual = load[...]
    smoothed = smooth(residual)
    wait_barrier()
    sum_y[0, me_y, :, :cv] = restrict(residual)
    sum_y[0, me_y, :, cv : cv + 128] = pack([per_load(residual * smoothed)])

    for turn in range(ITERS):
        for n in others:

            @pl.when(jnp.logical_not(neighbour(n)[2]))
            def _():
                ghost[turn, n] = jnp.zeros((ROWS, DOF), BF16)
                back_recv[turn, n] = jnp.zeros((ROWS, DOF), BF16)

    for n in range(9):
        wide[n * SPAN] = jnp.zeros((16, PAIR), F32)
        wide[n * SPAN + SPAN - 1] = jnp.zeros((16, PAIR), F32)
    for z in range(BZ):
        terms[z * SLOTS + NS] = jnp.zeros((NLOAD, DOF), F32)
    ones = ((iota((16, PAIR), 1) < DOF) == (iota((16, PAIR), 0) < NLOAD)).astype(F32)
    for z in range(BZ):
        row_sum[z] = dot_t(ones, row_in[z], HI)
    for s in range(NS):
        both = col_in[s]
        col[s] = (both + pltpu.roll(both, DOF, 1))[:, :DOF]

    summed = all_sum(0, cv + 128)
    coarse = summed[:, :cv]
    local_energy = pick(summed[:, cv:], 0)
    energy = local_energy + jnp.sum(coarse * coarse, axis=1, keepdims=True)
    direction = smoothed + prolong(coarse)
    shift = (iota((DOF, PAIR), 1) == iota((DOF, PAIR), 0) + DOF).astype(BF16)
    stay = (iota((DOF, PAIR), 1) == iota((DOF, PAIR), 0)).astype(BF16)

    def tiled(value):
        return jnp.concatenate([value] * BZ, axis=0)

    def apply_operator(turn, rounded):
        ghost[turn, 4] = rounded
        start, finish_recv, finish_send = exchange(
            turn, lambda n: ghost.at[turn, 4], ghost, halo_send_sem, halo_recv_sem
        )
        for n in others:
            start(n)
        even = dot(rounded, to_even.astype(BF16))
        odd = dot(rounded, to_odd.astype(BF16))
        even_img[...] = even
        odd_img[...] = odd
        if turn == 0:
            load_w.wait()

        @pl.loop(0, BZ)
        def _(z):
            rows = pl.ds(pl.multiple_of(z * NLOAD, NLOAD), NLOAD)
            both = jnp.concatenate([even_img[rows, :], odd_img[rows, :]], axis=0).astype(BF16)
            product = dot(both, w[z])
            for s in range(NS):
                part = product[:, s * PAIR : (s + 1) * PAIR]
                terms[z * SLOTS + s] = (part[:NLOAD] + pltpu.roll(part[NLOAD:], DOF, 1))[:, :DOF]

        for n in others:
            finish_recv(n)

        @pl.loop(0, 9)
        def _(n):
            field = ghost[turn, n]
            top, bottom = dot(field, stay), dot(field, shift)
            for z in range(BZ):
                rows = slice(z * NLOAD, (z + 1) * NLOAD)
                wide[n * SPAN + 1 + z, :NLOAD, :] = top[rows]
                wide[n * SPAN + 1 + z, NLOAD:, :] = bottom[rows]

        @pl.loop(0, BZ)
        def _(z):
            for s in range(NS):
                at = codes[z * NS + s]
                near = wide[at]
                lhs[z, :, s * PAIR : (s + 1) * PAIR] = near.astype(BF16)
                terms[z * SLOTS + s] = (
                    col[s, pl.ds(z, 1), :] * near[:NLOAD, :DOF] - terms[z * SLOTS + s]
                )

        def pooled(n, z):
            total = None
            for b in range(3):
                part = terms[pool_at[(n * BZ + z) * 3 + b]]
                total = part if total is None else total + part
            return total

        start, finish_back, finish_back_send = exchange(
            turn, lambda n: back_send.at[turn, n], back_recv, back_send_sem, back_recv_sem
        )
        for n in others:

            @pl.loop(0, BZ // 2)
            def _(z2):
                both = jnp.concatenate([pooled(n, z2 * 2), pooled(n, z2 * 2 + 1)], axis=0)
                back_send[turn, n, pl.ds(pl.multiple_of(z2 * 16, 16), 16), :] = both.astype(BF16)

            start(n)

        @pl.loop(0, BZ)
        def _(z):
            rows = pl.ds(pl.multiple_of(z * NLOAD, NLOAD), NLOAD)
            own = wide[4 * SPAN + 1 + z].astype(BF16)
            out = dot_t(own, self_in[z]) - dot_t(lhs[z], w[z])
            both = jnp.concatenate([even_img[rows, :], odd_img[rows, :]], axis=0)
            out = out + row_sum[z] * both
            even_img[rows, :] = out[:NLOAD]
            odd_img[rows, :] = out[NLOAD:]
            image[rows, :] = pooled(4, z)

        out = image[...] + dot(even_img[...], from_even, HI) + dot(odd_img[...], from_odd, HI)
        for n in others:
            finish_back(n)
            out = out + back_recv[turn, n].astype(F32)
        for n in others:
            finish_send(n)
            finish_back_send(n)
        return out

    out = apply_operator(0, direction.astype(BF16))
    smooth_out = smooth(out)
    sum_y[1, me_y, :, :cv] = restrict(out)
    sum_y[1, me_y, :, cv : cv + 128] = pack(
        [
            per_load(direction * out),
            per_load(residual * smooth_out + out * smoothed),
            per_load(out * smooth_out),
        ]
    )
    summed = all_sum(1, cv + 128)
    scalars = summed[:, cv:]
    step = energy / pick(scalars, 0)
    coarse = coarse - step * summed[:, :cv]
    local_energy = local_energy - step * pick(scalars, 1) + step * step * pick(scalars, 2)
    new_energy = local_energy + jnp.sum(coarse * coarse, axis=1, keepdims=True)
    step_all = tiled(step)
    moved = step_all * direction
    residual = residual - step_all * out
    smoothed = smoothed - step_all * smooth_out
    direction = smoothed + prolong(coarse) + tiled(new_energy / energy) * direction

    out = apply_operator(1, direction.astype(BF16))
    sum_y[2, me_y, :, :128] = pack([per_load(direction * out)])
    step_all = tiled(new_energy / pick(all_sum(2, 128), 0))
    disp_out[...] = moved + step_all * direction
    res_out[...] = residual - step_all * out


def per_device(load, bond, words, block_cols, self_flat, inv_flat, basis, factor):
    nx, ny = lax.axis_size("gx"), lax.axis_size("gy")
    cv = factor.shape[1]
    words = words[0, 0]
    both = jnp.stack([words & 255, words >> 8], axis=-1)
    flags = (
        both.reshape(BZ, NS, 32, 16).transpose(1, 0, 2, 3).reshape(NS, 256, 16).astype(BF16)
    )
    codes = block_cols[0, 0]
    z = jnp.arange(BZ, dtype=jnp.int32)[:, None]
    offset = (codes // SPAN) * 3 + codes % SPAN - z
    hit = offset[:, :, None] == jnp.arange(27, dtype=jnp.int32)
    slot = jnp.sum(jnp.where(hit, jnp.arange(NS, dtype=jnp.int32)[:, None] - NS, 0), axis=1) + NS
    table = jnp.pad((slot + z * SLOTS).reshape(BZ, 9, 3), ((1, 1), (0, 0), (0, 0)), constant_values=NS)
    pool_at = jnp.stack([table[2 - b : 2 - b + BZ, :, b] for b in range(3)], axis=-1)
    pool_at = pool_at.transpose(1, 0, 2).reshape(-1)

    w, col, row, self_pairs, inv_pairs = prepare(
        bond[0, 0].transpose(1, 0, 2), flags, self_flat[0, 0], inv_flat[0, 0]
    )
    vmem = pl.BlockSpec(memory_space=pltpu.VMEM)
    smem = pl.BlockSpec(memory_space=pltpu.SMEM)
    dma = pltpu.SemaphoreType.DMA
    disp, res = pl.pallas_call(
        functools.partial(main_kernel, nx, ny),
        in_specs=[smem, smem, vmem, pl.BlockSpec(memory_space=pl.ANY)] + [vmem] * 6,
        out_specs=[vmem, vmem],
        out_shape=[jax.ShapeDtypeStruct((ROWS, DOF), F32)] * 2,
        scratch_shapes=[
            pltpu.VMEM((BZ, HALF, NS * PAIR), BF16),
            pltpu.VMEM((NS, BZ, DOF), F32),
            pltpu.VMEM((BZ, 16, HALF), F32),
            pltpu.VMEM((ITERS, 9, ROWS, DOF), BF16),
            pltpu.VMEM((GHOSTS, 16, PAIR), F32),
            pltpu.VMEM((BZ, 16, NS * PAIR), BF16),
            pltpu.VMEM((BZ * SLOTS, NLOAD, DOF), F32),
            pltpu.VMEM((ITERS, 9, ROWS, DOF), BF16),
            pltpu.VMEM((ITERS, 9, ROWS, DOF), BF16),
            pltpu.VMEM((3, ny, NLOAD, cv + 128), F32),
            pltpu.VMEM((3, nx, NLOAD, cv + 128), F32),
            pltpu.VMEM((ROWS, DOF), F32),
            pltpu.VMEM((ROWS, HALF), F32),
            pltpu.VMEM((ROWS, HALF), F32),
            dma,
            dma((ITERS, 9)),
            dma((ITERS, 9)),
            dma((ITERS, 9)),
            dma((ITERS, 9)),
            dma((3, ny)),
            dma((3, ny)),
            dma((3, nx)),
            dma((3, nx)),
        ],
        compiler_params=pltpu.CompilerParams(
            collective_id=0, has_side_effects=True, vmem_limit_bytes=56 * 1024 * 1024
        ),
        name="conjugate_gradients",
    )(
        codes.reshape(-1),
        pool_at,
        load.reshape(ROWS, DOF),
        w,
        col,
        row,
        self_pairs,
        inv_pairs,
        basis[0, 0].transpose(1, 0, 2),
        factor,
    )
    shape = (1, 1, BZ, NLOAD, DOF)
    return disp.reshape(shape), res.reshape(shape)


def solution(mesh):
    in_specs = (
        P("gx", "gy", None, None, None),
        P("gx", "gy", None, None, None),
        P("gx", "gy", None, None, None, None),
        P("gx", "gy", None, None),
        P("gx", "gy", None, None),
        P("gx", "gy", None, None),
        P("gx", "gy", None, None, None),
        P(("gx", "gy"), None),
    )
    out_specs = (P("gx", "gy", None, None, None), P("gx", "gy", None, None, None))
    return jax.shard_map(
        per_device, mesh=mesh, in_specs=in_specs, out_specs=out_specs, check_vma=False
    )
```

```python
import functools

import jax
import jax.numpy as jnp
from jax import lax
from jax.experimental import pallas as pl
from jax.experimental.pallas import tpu as pltpu
from jax.sharding import PartitionSpec as P

DOF = 192
HALF = 96
PAIR = 384
NS = 13
BZ = 8
NLOAD = 8
ROWS = BZ * NLOAD
ITERS = 2
SPAN = BZ + 2
GHOSTS = 9 * SPAN
SLOTS = NS + 1
HI = lax.Precision.HIGHEST
F32 = jnp.float32
BF16 = jnp.bfloat16
MESH = pl.DeviceIdType.MESH


def iota(shape, axis):
    return lax.broadcasted_iota(jnp.int32, shape, axis)


def dot(a, b, precision=None):
    return lax.dot_general(
        a, b, (((1,), (0,)), ((), ())), precision=precision, preferred_element_type=F32
    )


def dot_t(a, b, precision=None):
    return lax.dot_general(
        a, b, (((1,), (1,)), ((), ())), precision=precision, preferred_element_type=F32
    )


def prepare_kernel(
    bond, words, self_flat, inv_flat, w_out, col_out, row_out, self_out, inv_hi, inv_lo, scr, place
):
    step = pl.program_id(0)

    def spread(read):
        @pl.loop(0, 36)
        def _(k8):
            for u in range(8):
                k = k8 * 8 + u
                scr[pl.ds(pl.multiple_of(k * 8, 8), 8), :] = read(pl.ds(pl.multiple_of(k * 128, 128), 128))

    @pl.when(step == 0)
    def _():
        row_out[...] = jnp.zeros_like(row_out)
        point, at = iota((512, 512), 0), iota((512, 512), 1)
        to = at % 256
        place[...] = (point == (to // 32) * 64 + (to % 32) * 2 + at // 256).astype(BF16)
        spread(lambda lanes: inv_flat[:, lanes])
        for z in range(BZ):
            for t in range(3):
                value = scr[pl.ds(t * 8 + z, HALF, stride=24), :]
                high = value.astype(BF16)
                inv_hi[z, :, t * 128 : (t + 1) * 128] = high
                inv_lo[z, :, t * 128 : (t + 1) * 128] = (value - high.astype(F32)).astype(BF16)
        spread(lambda lanes: self_flat[:, lanes].astype(F32))
        for z in range(BZ):
            for t in range(3):
                self_out[z, :, t * 128 : (t + 1) * 128] = scr[
                    pl.ds(t * 8 + z, HALF, stride=24), :
                ].astype(BF16)

    spread(lambda lanes: bond[0, :, lanes].astype(F32))
    lane = iota((16, PAIR), 1)
    column = lane % DOF % 64
    code = (lane // DOF) * 8 + (column % 16) // 8 * 4 + column // 16
    picker = (code == iota((16, PAIR), 0)).astype(BF16)
    packed = jnp.concatenate([words[z, 0] for z in range(BZ)], axis=1)
    halves = jnp.concatenate([packed & 255, packed >> 8], axis=0).astype(F32).astype(BF16)
    apart = dot(halves, place[...])
    flags = jnp.concatenate([apart[:, :256], apart[:, 256:]], axis=0).T.astype(BF16)
    picked = dot(flags, picker).astype(jnp.int32)
    lane_bit = jnp.left_shift(1, iota((1, PAIR), 1) % DOF % 8)
    keep = jnp.where((picked & lane_bit) != 0, 1.0, 0.0).astype(F32)
    for z in range(BZ):
        for t in range(3):
            lanes = slice(t * 128, (t + 1) * 128)
            mask = keep[z * 32 : (z + 1) * 32, lanes]
            part = scr[pl.ds(t * 8 + z, HALF, stride=24), :] * jnp.concatenate([mask] * 3, axis=0)
            w_out[z, :, lanes] = part.astype(BF16)
            row_out[z, :, lanes] += part
            col_out[0, z : z + 1, lanes] = jnp.sum(part, axis=0, keepdims=True)


def prepare(bond, words, self_flat, inv_flat):
    whole = lambda *shape: pl.BlockSpec(shape, lambda s: (0,) * len(shape))
    return pl.pallas_call(
        prepare_kernel,
        grid=(NS,),
        in_specs=[
            pl.BlockSpec((1, BZ, DOF * DOF), lambda s: (s, 0, 0)),
            pl.BlockSpec((BZ, 1, 4, 64), lambda s: (0, s, 0, 0)),
            whole(BZ, DOF * DOF),
            whole(BZ, DOF * DOF),
        ],
        out_specs=[
            pl.BlockSpec((BZ, HALF, PAIR), lambda s: (0, 0, s)),
            pl.BlockSpec((1, BZ, PAIR), lambda s: (s, 0, 0)),
            whole(BZ, HALF, PAIR),
            whole(BZ, HALF, PAIR),
            whole(BZ, HALF, PAIR),
            whole(BZ, HALF, PAIR),
        ],
        out_shape=[
            jax.ShapeDtypeStruct((BZ, HALF, NS * PAIR), BF16),
            jax.ShapeDtypeStruct((NS, BZ, PAIR), F32),
            jax.ShapeDtypeStruct((BZ, HALF, PAIR), F32),
            jax.ShapeDtypeStruct((BZ, HALF, PAIR), BF16),
            jax.ShapeDtypeStruct((BZ, HALF, PAIR), BF16),
            jax.ShapeDtypeStruct((BZ, HALF, PAIR), BF16),
        ],
        scratch_shapes=[pltpu.VMEM((288 * 8, 128), F32), pltpu.VMEM((512, 512), BF16)],
        compiler_params=pltpu.CompilerParams(vmem_limit_bytes=50 * 1024 * 1024),
        name="prepare",
    )(bond, words, self_flat, inv_flat)


def main_kernel(
    nx,
    ny,
    codes,
    pool_at,
    load,
    w_hbm,
    col_in,
    row_in,
    self_in,
    inv_high,
    inv_low,
    basis,
    factor,
    disp_out,
    res_out,
    w,
    col,
    row_sum,
    ghost,
    wide,
    lhs,
    terms,
    back_send,
    back_recv,
    sum_y,
    sum_x,
    image,
    even_img,
    odd_img,
    forward,
    w_sem,
    halo_send_sem,
    halo_recv_sem,
    back_send_sem,
    back_recv_sem,
    y_send_sem,
    y_recv_sem,
    x_send_sem,
    x_recv_sem,
):
    cv = factor.shape[1]
    me_x, me_y = lax.axis_index("gx"), lax.axis_index("gy")

    def neighbour(n):
        x, y = me_x + n // 3 - 1, me_y + n % 3 - 1
        return x, y, (x >= 0) & (x < nx) & (y >= 0) & (y < ny)

    others = [n for n in range(9) if n != 4]
    load_w = pltpu.make_async_copy(w_hbm, w, w_sem)
    load_w.start()
    barrier = pltpu.get_barrier_semaphore()
    for n in others:
        x, y, there = neighbour(n)

        @pl.when(there)
        def _():
            pl.semaphore_signal(barrier, inc=1, device_id=(x, y), device_id_type=MESH)

    for off in range(1, ny):
        pl.semaphore_signal(
            barrier, inc=1, device_id=(me_x, lax.rem(me_y + off, ny)), device_id_type=MESH
        )
    for off in range(1, nx):
        pl.semaphore_signal(
            barrier, inc=1, device_id=(lax.rem(me_x + off, nx), me_y), device_id_type=MESH
        )

    def wait_barrier():
        peers = nx + ny - 2
        for n in others:
            peers = peers + neighbour(n)[2].astype(jnp.int32)
        pl.semaphore_wait(barrier, peers)

    to_even = (iota((DOF, HALF), 0) == 2 * iota((DOF, HALF), 1)).astype(BF16)
    to_odd = (iota((DOF, HALF), 0) == 2 * iota((DOF, HALF), 1) + 1).astype(BF16)
    from_even = (iota((HALF, DOF), 1) == 2 * iota((HALF, DOF), 0)).astype(BF16)
    from_odd = (iota((HALF, DOF), 1) == 2 * iota((HALF, DOF), 0) + 1).astype(BF16)
    lane = iota((NLOAD, 128), 1)

    def per_load(product):
        total = jnp.sum(product.reshape(BZ, NLOAD, DOF), axis=0)
        return jnp.sum(total, axis=1, keepdims=True)

    def split(field):
        high = field.astype(BF16)
        return high, (field - high.astype(F32)).astype(BF16)

    def smooth(field):
        parts = jnp.concatenate(split(field), axis=0)
        even, odd = dot(parts, to_even), dot(parts, to_odd)
        out = []
        for z in range(BZ):
            high = slice(z * NLOAD, (z + 1) * NLOAD)
            low = slice(ROWS + z * NLOAD, ROWS + (z + 1) * NLOAD)
            both = jnp.concatenate([even[high], odd[high], even[low], odd[low]], axis=0).astype(BF16)
            first = dot(both, inv_high[z])
            product = first[:16] + first[16:] + dot(both[:16], inv_low[z])
            out.append((product[:NLOAD] + pltpu.roll(product[NLOAD:], DOF, 1))[:, :DOF])
        return jnp.concatenate(out, axis=0)

    def restrict(field):
        total = None
        for z in range(BZ):
            part = dot_t(field[z * NLOAD : (z + 1) * NLOAD], basis[z], HI)
            total = part if total is None else total + part
        return dot(total, factor[...], HI)

    def prolong(t):
        spread = dot_t(t, factor[...], HI)
        return jnp.concatenate([dot(spread, basis[z], HI) for z in range(BZ)], axis=0)

    def pack(values):
        out = jnp.zeros((NLOAD, 128), F32)
        for k, value in enumerate(values):
            out = jnp.where(lane == k, value, out)
        return out

    def pick(packed, k):
        return jnp.sum(jnp.where(lane == k, packed, 0.0), axis=1, keepdims=True)

    def all_sum(turn, width, beside=lambda: None):
        for buf, send_sem, recv_sem, me, size, axis in (
            (sum_y, y_send_sem, y_recv_sem, me_y, ny, 1),
            (sum_x, x_send_sem, x_recv_sem, me_x, nx, 0),
        ):
            copies = []
            for off in range(1, size):
                to = lax.rem(me + off, size)
                slot = buf.at[turn, me, :, pl.ds(0, width)]
                copy = pltpu.make_async_remote_copy(
                    src_ref=slot,
                    dst_ref=slot,
                    send_sem=send_sem.at[turn, off - 1],
                    recv_sem=recv_sem.at[turn, off - 1],
                    device_id=(me_x, to) if axis == 1 else (to, me_y),
                    device_id_type=MESH,
                )
                copy.start()
                copies.append(copy)
            if axis == 1:
                beside()
            for copy in copies:
                copy.wait_recv()
            for copy in copies:
                copy.wait_send()
            total = buf[turn, 0, :, :width]
            for j in range(1, size):
                total = total + buf[turn, j, :, :width]
            if axis == 1:
                sum_x[turn, me_x, :, :width] = total
        return total

    def exchange(turn, src, dst, send_sem, recv_sem):
        def copy_to(n):
            x, y, there = neighbour(n)
            copy = pltpu.make_async_remote_copy(
                src_ref=src(n),
                dst_ref=dst.at[turn, 8 - n],
                send_sem=send_sem.at[turn, n],
                recv_sem=recv_sem.at[turn, 8 - n],
                device_id=(x, y),
                device_id_type=MESH,
            )
            return copy, there

        def start(n):
            copy, there = copy_to(n)
            pl.when(there)(copy.start)

        def finish_recv(n):
            x, y, there = neighbour(n)
            arriving = pltpu.make_async_remote_copy(
                src_ref=src(n),
                dst_ref=dst.at[turn, n],
                send_sem=send_sem.at[turn, n],
                recv_sem=recv_sem.at[turn, n],
                device_id=(x, y),
                device_id_type=MESH,
            )
            pl.when(there)(arriving.wait_recv)

        def finish_send(n):
            copy, there = copy_to(n)
            pl.when(there)(copy.wait_send)

        return start, finish_recv, finish_send

    residual = load[...]
    smoothed = smooth(residual)
    wait_barrier()
    sum_y[0, me_y, :, :cv] = restrict(residual)
    sum_y[0, me_y, :, cv : cv + 128] = pack([per_load(residual * smoothed)])

    def set_up():
        for turn in range(ITERS):
            for n in others:

                @pl.when(jnp.logical_not(neighbour(n)[2]))
                def _():
                    ghost[turn, n] = jnp.zeros((ROWS, DOF), BF16)
                    back_recv[turn, n] = jnp.zeros((ROWS, DOF), BF16)

        for n in range(9):
            wide[n * SPAN] = jnp.zeros((16, PAIR), F32)
            wide[n * SPAN + SPAN - 1] = jnp.zeros((16, PAIR), F32)
        for z in range(BZ):
            terms[z * SLOTS + NS] = jnp.zeros((NLOAD, DOF), F32)
        ones = ((iota((16, PAIR), 1) < DOF) == (iota((16, PAIR), 0) < NLOAD)).astype(F32)
        sums = jnp.concatenate([dot_t(row_in[z], ones, HI) for z in range(BZ)], axis=1)
        row_sum[...] = sums.T
        for s in range(NS):
            both = col_in[s]
            col[s] = (both + pltpu.roll(both, DOF, 1))[:, :DOF]

    summed = all_sum(0, cv + 128, set_up)
    coarse = summed[:, :cv]
    local_energy = pick(summed[:, cv:], 0)
    energy = local_energy + jnp.sum(coarse * coarse, axis=1, keepdims=True)
    direction = smoothed + prolong(coarse)
    shift = (iota((DOF, PAIR), 1) == iota((DOF, PAIR), 0) + DOF).astype(BF16)
    stay = (iota((DOF, PAIR), 1) == iota((DOF, PAIR), 0)).astype(BF16)

    def tiled(value):
        return jnp.concatenate([value] * BZ, axis=0)

    def apply_operator(turn, rounded):
        ghost[turn, 4] = rounded
        start, finish_recv, finish_send = exchange(
            turn, lambda n: ghost.at[turn, 4], ghost, halo_send_sem, halo_recv_sem
        )
        for n in others:
            start(n)
        even = dot(rounded, to_even)
        odd = dot(rounded, to_odd)
        even_img[...] = even
        odd_img[...] = odd
        if turn == 0:
            load_w.wait()

        @pl.loop(0, BZ)
        def _(z):
            rows = pl.ds(pl.multiple_of(z * NLOAD, NLOAD), NLOAD)
            both = jnp.concatenate([even_img[rows, :], odd_img[rows, :]], axis=0).astype(BF16)
            product = dot(both, w[z])
            for s in range(NS):
                part = product[:, s * PAIR : (s + 1) * PAIR]
                terms[z * SLOTS + s] = (part[:NLOAD] + pltpu.roll(part[NLOAD:], DOF, 1))[:, :DOF]

        for n in others:
            finish_recv(n)

        @pl.loop(0, 9)
        def _(n):
            field = ghost[turn, n]
            top, bottom = dot(field, stay), dot(field, shift)
            for z in range(BZ):
                rows = slice(z * NLOAD, (z + 1) * NLOAD)
                wide[n * SPAN + 1 + z, :NLOAD, :] = top[rows]
                wide[n * SPAN + 1 + z, NLOAD:, :] = bottom[rows]

        @pl.loop(0, BZ)
        def _(z):
            for s in range(NS):
                at = codes[z * NS + s]
                near = wide[at]
                lhs[z, :, s * PAIR : (s + 1) * PAIR] = near.astype(BF16)
                terms[z * SLOTS + s] = (
                    col[s, pl.ds(z, 1), :] * near[:NLOAD, :DOF] - terms[z * SLOTS + s]
                )

        def pooled(n, z):
            total = None
            for b in range(3):
                part = terms[pool_at[(n * BZ + z) * 3 + b]]
                total = part if total is None else total + part
            return total

        start, finish_back, finish_back_send = exchange(
            turn, lambda n: back_send.at[turn, n], back_recv, back_send_sem, back_recv_sem
        )
        for n in others:

            @pl.loop(0, BZ // 2)
            def _(z2):
                both = jnp.concatenate([pooled(n, z2 * 2), pooled(n, z2 * 2 + 1)], axis=0)
                back_send[turn, n, pl.ds(pl.multiple_of(z2 * 16, 16), 16), :] = both.astype(BF16)

            start(n)

        @pl.loop(0, BZ)
        def _(z):
            rows = pl.ds(pl.multiple_of(z * NLOAD, NLOAD), NLOAD)
            own = wide[4 * SPAN + 1 + z].astype(BF16)
            forward[z] = dot_t(self_in[z], own) - dot_t(w[z], lhs[z])
            image[rows, :] = pooled(4, z)

        both = jnp.concatenate([forward[z] for z in range(BZ)], axis=1).T.reshape(BZ, 2, NLOAD, HALF)
        rates = row_sum[...].reshape(BZ, 2, NLOAD, HALF)
        out = image[...]
        for half, source, into in ((0, even_img, from_even), (1, odd_img, from_odd)):
            value = both[:, half].reshape(ROWS, HALF) + rates[:, half].reshape(ROWS, HALF) * source[...]
            high, rest = split(value)
            low = (value - high.astype(F32) - rest.astype(F32)).astype(BF16)
            for part in (low, rest, high):
                out = out + dot(part, into)
        for n in others:
            finish_back(n)
            out = out + back_recv[turn, n].astype(F32)
        for n in others:
            finish_send(n)
            finish_back_send(n)
        return out

    out = apply_operator(0, direction.astype(BF16))
    smooth_out = smooth(out)
    sum_y[1, me_y, :, :cv] = restrict(out)
    sum_y[1, me_y, :, cv : cv + 128] = pack(
        [
            per_load(direction * out),
            per_load(residual * smooth_out + out * smoothed),
            per_load(out * smooth_out),
        ]
    )
    summed = all_sum(1, cv + 128)
    scalars = summed[:, cv:]
    step = energy / pick(scalars, 0)
    coarse = coarse - step * summed[:, :cv]
    local_energy = local_energy - step * pick(scalars, 1) + step * step * pick(scalars, 2)
    new_energy = local_energy + jnp.sum(coarse * coarse, axis=1, keepdims=True)
    step_all = tiled(step)
    moved = step_all * direction
    residual = residual - step_all * out
    smoothed = smoothed - step_all * smooth_out
    direction = smoothed + prolong(coarse) + tiled(new_energy / energy) * direction

    out = apply_operator(1, direction.astype(BF16))
    sum_y[2, me_y, :, :128] = pack([per_load(direction * out)])
    step_all = tiled(new_energy / pick(all_sum(2, 128), 0))
    disp_out[...] = moved + step_all * direction
    res_out[...] = residual - step_all * out


def per_device(load, bond, words, block_cols, self_flat, inv_flat, basis, factor):
    nx, ny = lax.axis_size("gx"), lax.axis_size("gy")
    cv = factor.shape[1]
    codes = block_cols[0, 0]
    z = jnp.arange(BZ, dtype=jnp.int32)[:, None]
    offset = (codes // SPAN) * 3 + codes % SPAN - z
    hit = offset[:, :, None] == jnp.arange(27, dtype=jnp.int32)
    slot = jnp.sum(jnp.where(hit, jnp.arange(NS, dtype=jnp.int32)[:, None] - NS, 0), axis=1) + NS
    table = jnp.pad((slot + z * SLOTS).reshape(BZ, 9, 3), ((1, 1), (0, 0), (0, 0)), constant_values=NS)
    pool_at = jnp.stack([table[2 - b : 2 - b + BZ, :, b] for b in range(3)], axis=-1)
    pool_at = pool_at.transpose(1, 0, 2).reshape(-1)

    w, col, row, self_pairs, inv_high, inv_low = prepare(
        bond[0, 0].transpose(1, 0, 2), words[0, 0].transpose(0, 1, 3, 2), self_flat[0, 0], inv_flat[0, 0]
    )
    vmem = pl.BlockSpec(memory_space=pltpu.VMEM)
    smem = pl.BlockSpec(memory_space=pltpu.SMEM)
    dma = pltpu.SemaphoreType.DMA
    disp, res = pl.pallas_call(
        functools.partial(main_kernel, nx, ny),
        in_specs=[smem, smem, vmem, pl.BlockSpec(memory_space=pl.ANY)] + [vmem] * 7,
        out_specs=[vmem, vmem],
        out_shape=[jax.ShapeDtypeStruct((ROWS, DOF), F32)] * 2,
        scratch_shapes=[
            pltpu.VMEM((BZ, HALF, NS * PAIR), BF16),
            pltpu.VMEM((NS, BZ, DOF), F32),
            pltpu.VMEM((BZ * 16, HALF), F32),
            pltpu.VMEM((ITERS, 9, ROWS, DOF), BF16),
            pltpu.VMEM((GHOSTS, 16, PAIR), F32),
            pltpu.VMEM((BZ, 16, NS * PAIR), BF16),
            pltpu.VMEM((BZ * SLOTS, NLOAD, DOF), F32),
            pltpu.VMEM((ITERS, 9, ROWS, DOF), BF16),
            pltpu.VMEM((ITERS, 9, ROWS, DOF), BF16),
            pltpu.VMEM((3, ny, NLOAD, cv + 128), F32),
            pltpu.VMEM((3, nx, NLOAD, cv + 128), F32),
            pltpu.VMEM((ROWS, DOF), F32),
            pltpu.VMEM((ROWS, HALF), F32),
            pltpu.VMEM((ROWS, HALF), F32),
            pltpu.VMEM((BZ, HALF, 16), F32),
            dma,
            dma((ITERS, 9)),
            dma((ITERS, 9)),
            dma((ITERS, 9)),
            dma((ITERS, 9)),
            dma((3, ny)),
            dma((3, ny)),
            dma((3, nx)),
            dma((3, nx)),
        ],
        compiler_params=pltpu.CompilerParams(
            collective_id=0, has_side_effects=True, vmem_limit_bytes=28 * 1024 * 1024
        ),
        name="conjugate_gradients",
    )(
        codes.reshape(-1),
        pool_at,
        load.reshape(ROWS, DOF),
        w,
        col,
        row,
        self_pairs,
        inv_high,
        inv_low,
        basis[0, 0].transpose(1, 0, 2),
        factor,
    )
    shape = (1, 1, BZ, NLOAD, DOF)
    return disp.reshape(shape), res.reshape(shape)


def solution(mesh):
    in_specs = (
        P("gx", "gy", None, None, None),
        P("gx", "gy", None, None, None),
        P("gx", "gy", None, None, None, None),
        P("gx", "gy", None, None),
        P("gx", "gy", None, None),
        P("gx", "gy", None, None),
        P("gx", "gy", None, None, None),
        P(("gx", "gy"), None),
    )
    out_specs = (P("gx", "gy", None, None, None), P("gx", "gy", None, None, None))
    return jax.shard_map(
        per_device, mesh=mesh, in_specs=in_specs, out_specs=out_specs, check_vma=False
    )
```

```python
import functools

import jax
import jax.numpy as jnp
from jax import lax
from jax.experimental import pallas as pl
from jax.experimental.pallas import tpu as pltpu
from jax.sharding import PartitionSpec as P

DOF = 192
HALF = 96
PAIR = 384
NS = 13
BZ = 8
NLOAD = 8
ROWS = BZ * NLOAD
ITERS = 2
SPAN = BZ + 2
GHOSTS = 9 * SPAN
SLOTS = NS + 1
HI = lax.Precision.HIGHEST
F32 = jnp.float32
BF16 = jnp.bfloat16
MESH = pl.DeviceIdType.MESH


def iota(shape, axis):
    return lax.broadcasted_iota(jnp.int32, shape, axis)


def dot(a, b, precision=None):
    return lax.dot_general(
        a, b, (((1,), (0,)), ((), ())), precision=precision, preferred_element_type=F32
    )


def dot_t(a, b, precision=None):
    return lax.dot_general(
        a, b, (((1,), (1,)), ((), ())), precision=precision, preferred_element_type=F32
    )


def prepare_kernel(
    bond, words, self_flat, inv_flat, w_out, col_out, self_out, inv_hi, inv_lo, scr, place
):
    step = pl.program_id(0)

    def spread(read):
        @pl.loop(0, 36)
        def _(k8):
            for u in range(8):
                k = k8 * 8 + u
                scr[pl.ds(pl.multiple_of(k * 8, 8), 8), :] = read(pl.ds(pl.multiple_of(k * 128, 128), 128))

    @pl.when(step == 0)
    def _():
        point, at = iota((512, 512), 0), iota((512, 512), 1)
        to = at % 256
        place[...] = (point == (to // 32) * 64 + (to % 32) * 2 + at // 256).astype(BF16)
        spread(lambda lanes: inv_flat[:, lanes])
        for z in range(BZ):
            for t in range(3):
                value = scr[pl.ds(t * 8 + z, HALF, stride=24), :]
                high = value.astype(BF16)
                inv_hi[z, :, t * 128 : (t + 1) * 128] = high
                inv_lo[z, :, t * 128 : (t + 1) * 128] = (value - high.astype(F32)).astype(BF16)
        spread(lambda lanes: self_flat[:, lanes].astype(F32))
        for z in range(BZ):
            for t in range(3):
                self_out[z, :, t * 128 : (t + 1) * 128] = scr[
                    pl.ds(t * 8 + z, HALF, stride=24), :
                ].astype(BF16)

    for k in range(288):
        scr[k * 8 : k * 8 + 8, :] = bond[0, :, k * 128 : k * 128 + 128].astype(F32)
    lane = iota((16, PAIR), 1)
    column = lane % DOF % 64
    code = (lane // DOF) * 8 + (column % 16) // 8 * 4 + column // 16
    picker = (code == iota((16, PAIR), 0)).astype(BF16)
    packed = jnp.concatenate([words[z, 0] for z in range(BZ)], axis=1)
    halves = jnp.concatenate([packed & 255, packed >> 8], axis=0).astype(F32).astype(BF16)
    apart = dot(halves, place[...])
    flags = jnp.concatenate([apart[:, :256], apart[:, 256:]], axis=0).T.astype(BF16)
    picked = dot(flags, picker).astype(jnp.int32)
    lane_bit = jnp.left_shift(1, iota((1, PAIR), 1) % DOF % 8)
    keep = jnp.where((picked & lane_bit) != 0, 1.0, 0.0).astype(F32)
    for z in range(BZ):
        for t in range(3):
            lanes = slice(t * 128, (t + 1) * 128)
            mask = keep[z * 32 : (z + 1) * 32, lanes]
            part = scr[pl.ds(t * 8 + z, HALF, stride=24), :] * jnp.concatenate([mask] * 3, axis=0)
            w_out[z, :, lanes] = part.astype(BF16)
            col_out[0, z : z + 1, lanes] = jnp.sum(part, axis=0, keepdims=True)


def prepare(bond, words, self_flat, inv_flat):
    whole = lambda *shape: pl.BlockSpec(shape, lambda s: (0,) * len(shape))
    return pl.pallas_call(
        prepare_kernel,
        grid=(NS,),
        in_specs=[
            pl.BlockSpec((1, BZ, DOF * DOF), lambda s: (s, 0, 0)),
            pl.BlockSpec((BZ, 1, 4, 64), lambda s: (0, s, 0, 0)),
            whole(BZ, DOF * DOF),
            whole(BZ, DOF * DOF),
        ],
        out_specs=[
            pl.BlockSpec((BZ, HALF, PAIR), lambda s: (0, 0, s)),
            pl.BlockSpec((1, BZ, PAIR), lambda s: (s, 0, 0)),
            whole(BZ, HALF, PAIR),
            whole(BZ, HALF, PAIR),
            whole(BZ, HALF, PAIR),
        ],
        out_shape=[
            jax.ShapeDtypeStruct((BZ, HALF, NS * PAIR), BF16),
            jax.ShapeDtypeStruct((NS, BZ, PAIR), F32),
            jax.ShapeDtypeStruct((BZ, HALF, PAIR), BF16),
            jax.ShapeDtypeStruct((BZ, HALF, PAIR), BF16),
            jax.ShapeDtypeStruct((BZ, HALF, PAIR), BF16),
        ],
        scratch_shapes=[pltpu.VMEM((288 * 8, 128), F32), pltpu.VMEM((512, 512), BF16)],
        compiler_params=pltpu.CompilerParams(vmem_limit_bytes=59 * 1024 * 1024),
        name="prepare",
    )(bond, words, self_flat, inv_flat)


def main_kernel(
    nx,
    ny,
    codes,
    pool_at,
    load,
    w_hbm,
    col_in,
    self_in,
    inv_high,
    inv_low,
    basis,
    factor,
    disp_out,
    res_out,
    w,
    col,
    row_sum,
    ghost,
    wide,
    lhs,
    terms,
    back_send,
    back_recv,
    sum_y,
    sum_x,
    image,
    even_img,
    odd_img,
    forward,
    w_sem,
    halo_send_sem,
    halo_recv_sem,
    back_send_sem,
    back_recv_sem,
    y_send_sem,
    y_recv_sem,
    x_send_sem,
    x_recv_sem,
):
    cv = factor.shape[1]
    me_x, me_y = lax.axis_index("gx"), lax.axis_index("gy")

    def neighbour(n):
        x, y = me_x + n // 3 - 1, me_y + n % 3 - 1
        return x, y, (x >= 0) & (x < nx) & (y >= 0) & (y < ny)

    others = [n for n in range(9) if n != 4]
    load_w = pltpu.make_async_copy(w_hbm, w, w_sem)
    load_w.start()
    barrier = pltpu.get_barrier_semaphore()
    for n in others:
        x, y, there = neighbour(n)

        @pl.when(there)
        def _():
            pl.semaphore_signal(barrier, inc=1, device_id=(x, y), device_id_type=MESH)

    for off in range(1, ny):
        pl.semaphore_signal(
            barrier, inc=1, device_id=(me_x, lax.rem(me_y + off, ny)), device_id_type=MESH
        )
    for off in range(1, nx):
        pl.semaphore_signal(
            barrier, inc=1, device_id=(lax.rem(me_x + off, nx), me_y), device_id_type=MESH
        )

    def wait_barrier():
        peers = nx + ny - 2
        for n in others:
            peers = peers + neighbour(n)[2].astype(jnp.int32)
        pl.semaphore_wait(barrier, peers)

    to_even = (iota((DOF, HALF), 0) == 2 * iota((DOF, HALF), 1)).astype(BF16)
    to_odd = (iota((DOF, HALF), 0) == 2 * iota((DOF, HALF), 1) + 1).astype(BF16)
    from_even = (iota((HALF, DOF), 1) == 2 * iota((HALF, DOF), 0)).astype(BF16)
    from_odd = (iota((HALF, DOF), 1) == 2 * iota((HALF, DOF), 0) + 1).astype(BF16)
    lane = iota((NLOAD, 128), 1)

    def per_load(product):
        total = jnp.sum(product.reshape(BZ, NLOAD, DOF), axis=0)
        return jnp.sum(total, axis=1, keepdims=True)

    def split(field):
        high = field.astype(BF16)
        return high, (field - high.astype(F32)).astype(BF16)

    def smooth(field):
        parts = jnp.concatenate(split(field), axis=0)
        even, odd = dot(parts, to_even), dot(parts, to_odd)
        out = []
        for z in range(BZ):
            high = slice(z * NLOAD, (z + 1) * NLOAD)
            low = slice(ROWS + z * NLOAD, ROWS + (z + 1) * NLOAD)
            both = jnp.concatenate([even[high], odd[high], even[low], odd[low]], axis=0).astype(BF16)
            first = dot(both, inv_high[z])
            product = first[:16] + first[16:] + dot(both[:16], inv_low[z])
            out.append((product[:NLOAD] + pltpu.roll(product[NLOAD:], DOF, 1))[:, :DOF])
        return jnp.concatenate(out, axis=0)

    def restrict(field):
        total = None
        for z in range(BZ):
            part = dot_t(field[z * NLOAD : (z + 1) * NLOAD], basis[z], HI)
            total = part if total is None else total + part
        return dot(total, factor[...], HI)

    def prolong(t):
        spread = dot_t(t, factor[...], HI)
        return jnp.concatenate([dot(spread, basis[z], HI) for z in range(BZ)], axis=0)

    def pack(values):
        out = jnp.zeros((NLOAD, 128), F32)
        for k, value in enumerate(values):
            out = jnp.where(lane == k, value, out)
        return out

    def pick(packed, k):
        return jnp.sum(jnp.where(lane == k, packed, 0.0), axis=1, keepdims=True)

    sent = []

    def all_sum(turn, width, beside=lambda: None):
        for buf, send_sem, recv_sem, me, size, axis in (
            (sum_y, y_send_sem, y_recv_sem, me_y, ny, 1),
            (sum_x, x_send_sem, x_recv_sem, me_x, nx, 0),
        ):
            copies = []
            for off in range(1, size):
                to = lax.rem(me + off, size)
                slot = buf.at[turn, me, :, pl.ds(0, width)]
                copy = pltpu.make_async_remote_copy(
                    src_ref=slot,
                    dst_ref=slot,
                    send_sem=send_sem.at[turn, off - 1],
                    recv_sem=recv_sem.at[turn, off - 1],
                    device_id=(me_x, to) if axis == 1 else (to, me_y),
                    device_id_type=MESH,
                )
                copy.start()
                copies.append(copy)
            if axis == 1:
                beside()
            for copy in copies:
                copy.wait_recv()
            sent.extend(copies)
            total = buf[turn, 0, :, :width]
            for j in range(1, size):
                total = total + buf[turn, j, :, :width]
            if axis == 1:
                sum_x[turn, me_x, :, :width] = total
        return total

    def exchange(turn, src, dst, send_sem, recv_sem):
        def copy_to(n):
            x, y, there = neighbour(n)
            copy = pltpu.make_async_remote_copy(
                src_ref=src(n),
                dst_ref=dst.at[turn, 8 - n],
                send_sem=send_sem.at[turn, n],
                recv_sem=recv_sem.at[turn, 8 - n],
                device_id=(x, y),
                device_id_type=MESH,
            )
            return copy, there

        def start(n):
            copy, there = copy_to(n)
            pl.when(there)(copy.start)

        def finish_recv(n):
            x, y, there = neighbour(n)
            arriving = pltpu.make_async_remote_copy(
                src_ref=src(n),
                dst_ref=dst.at[turn, n],
                send_sem=send_sem.at[turn, n],
                recv_sem=recv_sem.at[turn, n],
                device_id=(x, y),
                device_id_type=MESH,
            )
            pl.when(there)(arriving.wait_recv)

        def finish_send(n):
            copy, there = copy_to(n)
            pl.when(there)(copy.wait_send)

        return start, finish_recv, finish_send

    residual = load[...]
    smoothed = smooth(residual)
    wait_barrier()
    sum_y[0, me_y, :, :cv] = restrict(residual)
    sum_y[0, me_y, :, cv : cv + 128] = pack([per_load(residual * smoothed)])

    def set_up():
        for turn in range(ITERS):
            for n in others:

                @pl.when(jnp.logical_not(neighbour(n)[2]))
                def _():
                    ghost[turn, n] = jnp.zeros((ROWS, DOF), BF16)
                    back_recv[turn, n] = jnp.zeros((ROWS, DOF), BF16)

        for n in range(9):
            wide[n * SPAN] = jnp.zeros((16, PAIR), F32)
            wide[n * SPAN + SPAN - 1] = jnp.zeros((16, PAIR), F32)
        for z in range(BZ):
            terms[z * SLOTS + NS] = jnp.zeros((NLOAD, DOF), F32)
        every = (16, NS * PAIR)
        ones = ((iota(every, 1) % PAIR < DOF) == (iota(every, 0) < NLOAD)).astype(F32).astype(BF16)
        load_w.wait()
        sums = jnp.concatenate([dot_t(w[z], ones) for z in range(BZ)], axis=1)
        row_sum[...] = sums.T
        for s in range(NS):
            both = col_in[s]
            col[s] = (both + pltpu.roll(both, DOF, 1))[:, :DOF]

    summed = all_sum(0, cv + 128, set_up)
    coarse = summed[:, :cv]
    local_energy = pick(summed[:, cv:], 0)
    energy = local_energy + jnp.sum(coarse * coarse, axis=1, keepdims=True)
    direction = smoothed + prolong(coarse)
    shift = (iota((DOF, PAIR), 1) == iota((DOF, PAIR), 0) + DOF).astype(BF16)
    stay = (iota((DOF, PAIR), 1) == iota((DOF, PAIR), 0)).astype(BF16)

    def tiled(value):
        return jnp.concatenate([value] * BZ, axis=0)

    def apply_operator(turn, rounded):
        ghost[turn, 4] = rounded
        start, finish_recv, finish_send = exchange(
            turn, lambda n: ghost.at[turn, 4], ghost, halo_send_sem, halo_recv_sem
        )
        for n in others:
            start(n)
        even = dot(rounded, to_even)
        odd = dot(rounded, to_odd)
        even_img[...] = even
        odd_img[...] = odd

        @pl.loop(0, BZ)
        def _(z):
            rows = pl.ds(pl.multiple_of(z * NLOAD, NLOAD), NLOAD)
            both = jnp.concatenate([even_img[rows, :], odd_img[rows, :]], axis=0).astype(BF16)
            product = dot(both, w[z])
            for s in range(NS):
                part = product[:, s * PAIR : (s + 1) * PAIR]
                terms[z * SLOTS + s] = (part[:NLOAD] + pltpu.roll(part[NLOAD:], DOF, 1))[:, :DOF]

        for n in others:
            finish_recv(n)

        @pl.loop(0, 9)
        def _(n):
            field = ghost[turn, n]
            top, bottom = dot(field, stay), dot(field, shift)
            for z in range(BZ):
                rows = slice(z * NLOAD, (z + 1) * NLOAD)
                wide[n * SPAN + 1 + z, :NLOAD, :] = top[rows]
                wide[n * SPAN + 1 + z, NLOAD:, :] = bottom[rows]

        @pl.loop(0, BZ)
        def _(z):
            for s in range(NS):
                at = codes[z * NS + s]
                near = wide[at]
                lhs[z, :, s * PAIR : (s + 1) * PAIR] = near.astype(BF16)
                terms[z * SLOTS + s] = (
                    col[s, pl.ds(z, 1), :] * near[:NLOAD, :DOF] - terms[z * SLOTS + s]
                )

        def pooled(n, z):
            total = None
            for b in range(3):
                part = terms[pool_at[(n * BZ + z) * 3 + b]]
                total = part if total is None else total + part
            return total

        start, finish_back, finish_back_send = exchange(
            turn, lambda n: back_send.at[turn, n], back_recv, back_send_sem, back_recv_sem
        )
        for n in others:

            @pl.loop(0, BZ // 2)
            def _(z2):
                both = jnp.concatenate([pooled(n, z2 * 2), pooled(n, z2 * 2 + 1)], axis=0)
                back_send[turn, n, pl.ds(pl.multiple_of(z2 * 16, 16), 16), :] = both.astype(BF16)

            start(n)

        @pl.loop(0, BZ)
        def _(z):
            rows = pl.ds(pl.multiple_of(z * NLOAD, NLOAD), NLOAD)
            own = wide[4 * SPAN + 1 + z].astype(BF16)
            forward[z] = dot_t(self_in[z], own) - dot_t(w[z], lhs[z])
            image[rows, :] = pooled(4, z)

        both = jnp.concatenate([forward[z] for z in range(BZ)], axis=1).T.reshape(BZ, 2, NLOAD, HALF)
        rates = row_sum[...].reshape(BZ, 2, NLOAD, HALF)
        out = image[...]
        for half, source, into in ((0, even_img, from_even), (1, odd_img, from_odd)):
            value = both[:, half].reshape(ROWS, HALF) + rates[:, half].reshape(ROWS, HALF) * source[...]
            high, rest = split(value)
            low = (value - high.astype(F32) - rest.astype(F32)).astype(BF16)
            for part in (low, rest, high):
                out = out + dot(part, into)
        for n in others:
            finish_back(n)
            out = out + back_recv[turn, n].astype(F32)
        for n in others:
            finish_send(n)
            finish_back_send(n)
        return out

    out = apply_operator(0, direction.astype(BF16))
    smooth_out = smooth(out)
    sum_y[1, me_y, :, :cv] = restrict(out)
    sum_y[1, me_y, :, cv : cv + 128] = pack(
        [
            per_load(direction * out),
            per_load(residual * smooth_out + out * smoothed),
            per_load(out * smooth_out),
        ]
    )
    summed = all_sum(1, cv + 128)
    scalars = summed[:, cv:]
    step = energy / pick(scalars, 0)
    coarse = coarse - step * summed[:, :cv]
    local_energy = local_energy - step * pick(scalars, 1) + step * step * pick(scalars, 2)
    new_energy = local_energy + jnp.sum(coarse * coarse, axis=1, keepdims=True)
    step_all = tiled(step)
    moved = step_all * direction
    residual = residual - step_all * out
    smoothed = smoothed - step_all * smooth_out
    direction = smoothed + prolong(coarse) + tiled(new_energy / energy) * direction

    out = apply_operator(1, direction.astype(BF16))
    sum_y[2, me_y, :, :128] = pack([per_load(direction * out)])
    step_all = tiled(new_energy / pick(all_sum(2, 128), 0))
    disp_out[...] = moved + step_all * direction
    res_out[...] = residual - step_all * out
    for copy in sent:
        copy.wait_send()


def per_device(load, bond, words, block_cols, self_flat, inv_flat, basis, factor):
    nx, ny = lax.axis_size("gx"), lax.axis_size("gy")
    cv = factor.shape[1]
    codes = block_cols[0, 0]
    z = jnp.arange(BZ, dtype=jnp.int32)[:, None]
    offset = (codes // SPAN) * 3 + codes % SPAN - z
    hit = offset[:, :, None] == jnp.arange(27, dtype=jnp.int32)
    slot = jnp.sum(jnp.where(hit, jnp.arange(NS, dtype=jnp.int32)[:, None] - NS, 0), axis=1) + NS
    table = jnp.pad((slot + z * SLOTS).reshape(BZ, 9, 3), ((1, 1), (0, 0), (0, 0)), constant_values=NS)
    pool_at = jnp.stack([table[2 - b : 2 - b + BZ, :, b] for b in range(3)], axis=-1)
    pool_at = pool_at.transpose(1, 0, 2).reshape(-1)

    w, col, self_pairs, inv_high, inv_low = prepare(
        bond[0, 0].transpose(1, 0, 2), words[0, 0].transpose(0, 1, 3, 2), self_flat[0, 0], inv_flat[0, 0]
    )
    vmem = pl.BlockSpec(memory_space=pltpu.VMEM)
    smem = pl.BlockSpec(memory_space=pltpu.SMEM)
    dma = pltpu.SemaphoreType.DMA
    disp, res = pl.pallas_call(
        functools.partial(main_kernel, nx, ny),
        in_specs=[smem, smem, vmem, pl.BlockSpec(memory_space=pl.ANY)] + [vmem] * 6,
        out_specs=[vmem, vmem],
        out_shape=[jax.ShapeDtypeStruct((ROWS, DOF), F32)] * 2,
        scratch_shapes=[
            pltpu.VMEM((BZ, HALF, NS * PAIR), BF16),
            pltpu.VMEM((NS, BZ, DOF), F32),
            pltpu.VMEM((BZ * 16, HALF), F32),
            pltpu.VMEM((ITERS, 9, ROWS, DOF), BF16),
            pltpu.VMEM((GHOSTS, 16, PAIR), F32),
            pltpu.VMEM((BZ, 16, NS * PAIR), BF16),
            pltpu.VMEM((BZ * SLOTS, NLOAD, DOF), F32),
            pltpu.VMEM((ITERS, 9, ROWS, DOF), BF16),
            pltpu.VMEM((ITERS, 9, ROWS, DOF), BF16),
            pltpu.VMEM((3, ny, NLOAD, cv + 128), F32),
            pltpu.VMEM((3, nx, NLOAD, cv + 128), F32),
            pltpu.VMEM((ROWS, DOF), F32),
            pltpu.VMEM((ROWS, HALF), F32),
            pltpu.VMEM((ROWS, HALF), F32),
            pltpu.VMEM((BZ, HALF, 16), F32),
            dma,
            dma((ITERS, 9)),
            dma((ITERS, 9)),
            dma((ITERS, 9)),
            dma((ITERS, 9)),
            dma((3, ny)),
            dma((3, ny)),
            dma((3, nx)),
            dma((3, nx)),
        ],
        compiler_params=pltpu.CompilerParams(
            collective_id=0, has_side_effects=True, vmem_limit_bytes=59 * 1024 * 1024
        ),
        name="conjugate_gradients",
    )(
        codes.reshape(-1),
        pool_at,
        load.reshape(ROWS, DOF),
        w,
        col,
        self_pairs,
        inv_high,
        inv_low,
        basis[0, 0].transpose(1, 0, 2),
        factor,
    )
    shape = (1, 1, BZ, NLOAD, DOF)
    return disp.reshape(shape), res.reshape(shape)


def solution(mesh):
    in_specs = (
        P("gx", "gy", None, None, None),
        P("gx", "gy", None, None, None),
        P("gx", "gy", None, None, None, None),
        P("gx", "gy", None, None),
        P("gx", "gy", None, None),
        P("gx", "gy", None, None),
        P("gx", "gy", None, None, None),
        P(("gx", "gy"), None),
    )
    out_specs = (P("gx", "gy", None, None, None), P("gx", "gy", None, None, None))
    return jax.shard_map(
        per_device, mesh=mesh, in_specs=in_specs, out_specs=out_specs, check_vma=False
    )
```
